256 devices in a mesh: occ: 128 (over z, y, x), aux: 2 (over core).
Axes of the slice: x: 4, y: 4, z: 8, core: 2. Of those that a mesh axis runs over, the one named last changes fastest.
Arguments:
- three_index: bfloat16 [2, 256, 1280, 1152], P('aux', None, 'occ'), may hold values from -0.8984375 to 0.8984375
- partners: int32 [256], replicated, may hold values from 0 to 255, each once
- vir_blocks: int32 [512, 2, 8], replicated, may hold values from 0 to 8, as said below
- fit_blocks: int32 [512, 2, 2, 8], P('occ', None, 'aux'), may hold values from 0 to 9, as said below
- block_counts: int32 [512, 2], P('occ'), may hold values from 1 to 8
- virt_energies: float32 [512, 1024], P('occ'), may hold values from 0.1 to 1.5
- occ_energies: float32 [256], replicated, may hold values from -1 to -0.25
Outputs:
- amplitudes: bfloat16 [512, 1024, 1024], P('occ', 'aux')
The draws below stay inside these ranges and needn't reach their ends.
Inputs may be any that keep to these rules, and one draw needn't show every extreme that they name: `vir_blocks`: each pair's 8 positions for one side are distinct. `fit_blocks`: each pair's 8 positions for one side and half are distinct.
All inputs are finite; a program needn't handle non-finite values.
Results may differ from the reference program's by a relative error of at most 0.001.
Values may be sent and summed in bfloat16 or wider, within the bound.
No kernel may reach another device: no remote copies, remote signals or barrier semaphores. Data moves between devices by JAX's collectives and lax.ppermute only.
A program may use at most 192 MiB of HBM per device.

```python
import math
import jax
import jax.numpy as jnp
from jax import lax

BLK = 128
OCC_DEV = 2
PARTNERS = 2
ODB = 9
VB = 8
OFB = 10
FB = 8
NOCC = 256
NPAIRS = 512
PV = 1024
ODV = 1152
HALF_AUX = 1280


def distinct_positions(key, lead, pool, count):
    scores = jax.random.randint(key, lead + (pool,), 0, 1 << 20, dtype=jnp.int32)
    scores = scores * pool + jnp.arange(pool, dtype=jnp.int32)
    order = jnp.argsort(scores, axis=-1, stable=True)
    return order[..., :count].astype(jnp.int32)


def draw_vir_blocks(key, part):
    return distinct_positions(jax.random.fold_in(key, 11), (NPAIRS, 2), ODB, VB)


def draw_fit_blocks(key, part):
    return distinct_positions(jax.random.fold_in(key, 23), (NPAIRS, 2, 2), OFB, FB)


def place_ends(array, rng, smallest, high):
    index_at = [jax.random.randint(jax.random.fold_in(rng, axis), (), 0, length) for axis, length in enumerate(array.shape)]
    longest = array.shape.index(max(array.shape))
    beside = index_at[:longest] + [(index_at[longest] + 1) % array.shape[longest]] + index_at[longest + 1:]
    return array.at[tuple(index_at)].set(smallest).at[tuple(beside)].set(high)


def levels(rng, shape, cuts, least, top_value):
    def one(position, blocks):
        draws = jax.random.uniform(jax.random.fold_in(jax.random.fold_in(rng, 6), position), (blocks,), jnp.float32, least / len(cuts), top_value / len(cuts))
        return jnp.repeat(jnp.exp(draws), shape[position] // blocks).reshape((-1,) + (1,) * (len(shape) - position - 1))

    factor_of = one(*cuts[0])
    for cut in cuts[1:]:
        factor_of = factor_of * one(*cut)
    return factor_of


def normal_values(own_key, shape, deviation, limit, cuts=(), kind=jnp.bfloat16):
    values = jax.random.normal(own_key, shape, jnp.float32) * deviation
    if len(cuts) > 0:
        values = levels(own_key, shape, cuts, -0.22, 0.18) * values
    return jnp.clip(values, min=-limit, max=limit).astype(kind)


def setup_inputs(seed: int = 0) -> dict:
    streams_of = jax.random.split(jax.random.key(seed), 8)
    return {
        "three_index": normal_values(streams_of[0], (2, NOCC, HALF_AUX, ODV), 0.15, 0.8984375, ((0, 2), (2, 128))),
        "partners": jax.random.permutation(streams_of[1], NOCC).astype(jnp.int32),
        "vir_blocks": draw_vir_blocks(jax.random.fold_in(streams_of[7], 71), 0),
        "fit_blocks": draw_fit_blocks(jax.random.fold_in(streams_of[7], 71), 0),
        "block_counts": place_ends(jax.random.randint(streams_of[4], (NPAIRS, 2), 1, VB + 1), jax.random.fold_in(streams_of[4], 1), 1, VB).astype(jnp.int32),
        "virt_energies": jnp.clip(jnp.exp(math.log(1.5) - 2.7080502 * jax.random.uniform(streams_of[5], (NPAIRS, PV), jnp.float32) ** levels(streams_of[5], (NPAIRS, PV), ((0, 128),), -0.2, 0.2)), 0.1, 1.5),
        "occ_energies": jnp.clip(jax.random.uniform(streams_of[6], (NOCC,), jnp.float32, -1.0, -0.25), -1.0, -0.25),
    }


def select_blocks(matrix, fit_pos, vir_pos):
    blocked = matrix.reshape(matrix.shape[0] // BLK, BLK, matrix.shape[1] // BLK, BLK)
    chosen = blocked[fit_pos][:, :, vir_pos, :]
    return chosen.reshape(fit_pos.shape[0], BLK, vir_pos.shape[0] * BLK)


def reference(three_index, partners, vir_blocks, fit_blocks, block_counts, virt_energies, occ_energies):
    pairs_dev = OCC_DEV * PARTNERS

    def one_pair(g):
        q = g // pairs_dev
        r = g % pairs_dev
        i = (q * OCC_DEV + r // PARTNERS).astype(jnp.int32)
        j = partners[(q * PARTNERS + r % PARTNERS).astype(jnp.int32)]
        live_fit = jnp.arange(FB, dtype=jnp.int32) < block_counts[g, 1]
        summed = jnp.zeros((VB * BLK, VB * BLK), jnp.float32)
        for c in range(2):
            left_side = select_blocks(three_index[c, i], fit_blocks[g, 0, c], vir_blocks[g, 0])
            left_side = jnp.where(live_fit[:, None, None], left_side, jnp.zeros((), three_index.dtype))
            left_side = left_side.reshape(FB * BLK, VB * BLK)
            right_side = select_blocks(three_index[c, j], fit_blocks[g, 1, c], vir_blocks[g, 1])
            right_side = right_side.reshape(FB * BLK, VB * BLK)
            summed = summed + jnp.dot(left_side.T, right_side, preferred_element_type=jnp.float32)
        energies = virt_energies[g]
        denominator = energies[:, None] + energies[None, :] - occ_energies[i] - occ_energies[j]
        live_rows = jnp.arange(VB * BLK, dtype=jnp.int32) < block_counts[g, 0] * BLK
        amplitude = jnp.where(live_rows[:, None] & live_rows[None, :], -summed / denominator, 0.0)
        return amplitude.astype(jnp.bfloat16)

    return lax.map(one_pair, jnp.arange(NPAIRS, dtype=jnp.int32))
```

```python
import functools

import jax
import jax.numpy as jnp
from jax import lax
from jax.experimental import pallas as pl
from jax.experimental.pallas import tpu as pltpu
from jax.sharding import PartitionSpec as P

BLK = 128
OCC_DEV = 2
PARTNERS = 2
ODB = 9
VB = 8
OFB = 10
FB = 8
LATE = 4
EARLY = ODB - LATE
ROWP = 5
HALF = BLK // 2
F32 = jnp.float32
BF16 = jnp.bfloat16

EARLY_UNITS = (
    [(0, c) for c in range(ODB)]
    + [(1, c) for c in range(ODB)]
    + [(2, c) for c in range(ODB)]
    + [(3, c) for c in range(EARLY)]
)
LATE_UNITS = [(3, c) for c in range(EARLY, ODB)]
EARLY_GROUPS = len(EARLY_UNITS) // 4
LATE_GROUPS = len(LATE_UNITS) // 4
VMEM_LIMIT = 60 * 1024 * 1024


def pack_kernel(pick_ref, rows_ref, early_ref, late_ref, spread):
    owners = early_ref.shape[0]
    for o in range(4):
        units = [(n, c) for n, (q, c) in enumerate(EARLY_UNITS + LATE_UNITS) if q == o]
        for w in range(2):
            picked = jnp.dot(
                pick_ref[o * owners : (o + 1) * owners, :],
                rows_ref[w],
                preferred_element_type=F32,
            )
            for n, c in units:
                spread[n // 4, pl.ds((n % 4) * 2 + w, owners, stride=8), :] = picked[
                    :, c * BLK : (c + 1) * BLK
                ]
    for g in range(EARLY_GROUPS):
        early_ref[:, 0, g] = spread[g].reshape(owners, 8, BLK).astype(BF16)
    for g in range(LATE_GROUPS):
        late_ref[:, 0, g] = spread[EARLY_GROUPS + g].reshape(owners, 8, BLK).astype(BF16)


def pack(pick, rows, owners):
    orbitals, width = rows.shape[1], rows.shape[2]
    groups = (EARLY_GROUPS, LATE_GROUPS)
    return pl.pallas_call(
        pack_kernel,
        grid=(ROWP,),
        in_specs=[
            pl.BlockSpec((4 * owners, orbitals), lambda r: (0, 0)),
            pl.BlockSpec((2, orbitals, width), lambda r: (r, 0, 0)),
        ],
        out_specs=[
            pl.BlockSpec((owners, 1, n, 8, BLK), lambda r: (0, r, 0, 0, 0)) for n in groups
        ],
        out_shape=[
            jax.ShapeDtypeStruct((owners, ROWP, n, 8, BLK), BF16) for n in groups
        ],
        scratch_shapes=[
            pltpu.VMEM((EARLY_GROUPS + LATE_GROUPS, owners * 8, BLK), F32)
        ],
        compiler_params=pltpu.CompilerParams(vmem_limit_bytes=VMEM_LIMIT),
        name="pack",
    )(pick, rows)


def unpack_kernel(order_ref, in_ref, *out_refs, targets):
    groups = in_ref.shape[1]
    for s in range(2):
        part = in_ref[s * 32 : (s + 1) * 32].astype(F32)
        for g in range(groups):
            rows = part[:, g].reshape(256, BLK).astype(BF16)
            sorted_rows = jnp.dot(order_ref[...], rows, preferred_element_type=F32)
            sorted_rows = sorted_rows.astype(BF16)
            for j in range(4):
                which, slot = targets[g * 4 + j]
                out_refs[which][slot, 0, s * HALF : (s + 1) * HALF, :] = sorted_rows[
                    j * HALF : (j + 1) * HALF
                ]


def unpack(order, arrived, counts, targets):
    pairs, groups = arrived.shape[0], arrived.shape[1]
    return pl.pallas_call(
        functools.partial(unpack_kernel, targets=targets),
        grid=(OFB,),
        in_specs=[
            pl.BlockSpec((256, 256), lambda f: (0, 0)),
            pl.BlockSpec((pairs // OFB, groups, 8, BLK), lambda f: (f, 0, 0, 0)),
        ],
        out_specs=[
            pl.BlockSpec((n, 1, BLK, BLK), lambda f: (0, f, 0, 0)) for n in counts
        ],
        out_shape=[jax.ShapeDtypeStruct((n, OFB, BLK, BLK), BF16) for n in counts],
        compiler_params=pltpu.CompilerParams(vmem_limit_bytes=VMEM_LIMIT),
        name="unpack",
    )(order, arrived)


def pair_kernel(
    vir_ref, fit_ref, count_ref, occ_ref, aux_ref, *refs, partner, right_parts
):
    lefts = refs[:2]
    rights = refs[2 : 2 + 2 * len(right_parts)]
    energy_ref, out_ref, left_mat, right_mat = refs[2 + 2 * len(right_parts) :]
    k = pl.program_id(0)
    p = k * PARTNERS + partner
    aux = aux_ref[0]
    fit_count = count_ref[p, 1]
    half_blocks = VB // 2
    for h in range(2):

        @pl.loop(0, FB)
        def _(f):
            at = pl.multiple_of((h * FB + f) * BLK, BLK)
            left_pos = fit_ref[h, p, 0, f]
            right_pos = fit_ref[h, p, 1, f]
            live = f < fit_count
            for v in range(half_blocks):
                c = vir_ref[p, 0, aux * half_blocks + v]
                block = lefts[h][c, left_pos]
                left_mat[pl.ds(at, BLK), v * BLK : (v + 1) * BLK] = jnp.where(
                    live, block, jnp.zeros_like(block)
                )
            for v in range(VB):
                c = vir_ref[p, 1, v]
                where = pl.ds(at, BLK), slice(v * BLK, (v + 1) * BLK)
                start = 0
                for part, size in enumerate(right_parts):
                    source = rights[2 * part + h]

                    @pl.when((c >= start) & (c < start + size))
                    def _(source=source, start=start):
                        right_mat[where] = source[c - start, right_pos]

                    start += size

    live_limit = count_ref[p, 0] * BLK
    occ_sum = (occ_ref[0, p], occ_ref[1, p])
    row_base = aux * half_blocks * BLK
    for v in range(half_blocks):
        row_id = row_base + v * BLK + lax.broadcasted_iota(jnp.int32, (BLK, 1), 0)
        at = pl.multiple_of(row_base + v * BLK, BLK)
        row_energy = energy_ref[0, :, pl.ds(at, BLK)].reshape(BLK, 1)
        product = lax.dot_general(
            left_mat[:, v * BLK : (v + 1) * BLK],
            right_mat[...],
            (((0,), (0,)), ((), ())),
            preferred_element_type=F32,
        )
        denominator = row_energy + energy_ref[0] - occ_sum[0] - occ_sum[1]
        col_id = lax.broadcasted_iota(jnp.int32, (1, VB * BLK), 1)
        live = (row_id < live_limit) & (col_id < live_limit)
        amplitude = jnp.where(live, -product / denominator, 0.0)
        out_ref[0, 0, v * BLK : (v + 1) * BLK, :] = amplitude.astype(BF16)


def pair_products(scalars, lefts, rights, energies, partner):
    right_parts = tuple(r[0].shape[0] for r in rights)
    width = VB * BLK
    left_spec = pl.BlockSpec((ODB, OFB, BLK, BLK), lambda k, *_: (k, 0, 0, 0))
    right_specs = [
        pl.BlockSpec((n, OFB, BLK, BLK), lambda k, *_: (0, 0, 0, 0))
        for n in right_parts
        for _ in range(2)
    ]
    return pl.pallas_call(
        functools.partial(pair_kernel, partner=partner, right_parts=right_parts),
        grid_spec=pltpu.PrefetchScalarGridSpec(
            num_scalar_prefetch=5,
            grid=(OCC_DEV,),
            in_specs=[left_spec, left_spec]
            + right_specs
            + [
                pl.BlockSpec(
                    (1, 1, width), lambda k, *_: (k * PARTNERS + partner, 0, 0)
                )
            ],
            out_specs=pl.BlockSpec((1, 1, width // 2, width), lambda k, *_: (k, 0, 0, 0)),
            scratch_shapes=[
                pltpu.VMEM((2 * FB * BLK, width // 2), BF16),
                pltpu.VMEM((2 * FB * BLK, width), BF16),
            ],
        ),
        out_shape=jax.ShapeDtypeStruct((OCC_DEV, 1, width // 2, width), BF16),
        compiler_params=pltpu.CompilerParams(vmem_limit_bytes=VMEM_LIMIT),
        name="pairs",
    )(*scalars, *lefts, *[x for r in rights for x in r], energies)


def per_device(
    three_index, partners, vir_blocks, fit_blocks, block_counts, virt_energies, occ_energies
):
    owners = lax.axis_size("occ")
    owner = lax.axis_index("occ")
    aux = lax.axis_index("aux")
    pairs_dev = OCC_DEV * PARTNERS
    swap = [(0, 1), (1, 0)]

    rows = jnp.transpose(three_index[0], (1, 0, 2))
    orbitals = jnp.arange(rows.shape[1], dtype=jnp.int32)
    wanted = jnp.concatenate(
        [orbitals.reshape(owners, OCC_DEV).T.reshape(-1), partners.reshape(owners, PARTNERS).T.reshape(-1)]
    )
    pick = (wanted[:, None] == orbitals[None, :]).astype(BF16)
    early, late = pack(pick, rows, owners)

    early = lax.all_to_all(early, "occ", 0, 0, tiled=True)
    late = lax.all_to_all(late, "occ", 0, 0, tiled=True)

    place = jnp.arange(256, dtype=jnp.int32)
    source = (place % HALF) // 2 * 8 + (place // HALF) * 2 + place % 2
    order = (source[:, None] == place[None, :]).astype(BF16)

    targets = [(0, o * ODB + c) for o in range(2) for c in range(ODB)]
    targets += [(1, c) for c in range(ODB)] + [(2, c) for c in range(EARLY)]
    flat = early.reshape(owners * ROWP, EARLY_GROUPS, 8, BLK)
    left, first, second = unpack(order, flat, (2 * ODB, ODB, EARLY), targets)
    flat = late.reshape(owners * ROWP, LATE_GROUPS, 8, BLK)
    (third,) = unpack(order, flat, (LATE,), [(0, c) for c in range(LATE)])

    def both(x):
        return x, lax.ppermute(x, "aux", swap)

    fit_own = fit_blocks[:, :, 0, :]
    fits = jnp.stack(both(fit_own))
    vir = lax.dynamic_slice_in_dim(vir_blocks, owner * pairs_dev, pairs_dev, 0)
    mine = lax.dynamic_slice_in_dim(occ_energies, owner * OCC_DEV, OCC_DEV, 0)
    partner_ids = lax.dynamic_slice_in_dim(partners, owner * PARTNERS, PARTNERS, 0)
    theirs = jnp.sum(
        jnp.where(partner_ids[:, None] == orbitals[None, :], occ_energies[None, :], 0.0), axis=1
    )
    occ_pair = jnp.stack(
        [jnp.repeat(mine, PARTNERS), jnp.concatenate([theirs] * OCC_DEV)]
    )
    scalars = (vir, fits, block_counts, occ_pair, aux.reshape(1))
    energies = virt_energies[:, None, :]

    lefts = both(left)
    out0 = pair_products(scalars, lefts, [both(first)], energies, 0)
    out1 = pair_products(scalars, lefts, [both(second), both(third)], energies, 1)
    out = jnp.concatenate([out0, out1], axis=1)
    return out.reshape(pairs_dev, VB * BLK // 2, VB * BLK)


def solution(mesh):
    return jax.shard_map(
        per_device,
        mesh=mesh,
        in_specs=(
            P("aux", None, "occ", None),
            P(),
            P(),
            P("occ", None, "aux", None),
            P("occ", None),
            P("occ", None),
            P(),
        ),
        out_specs=P("occ", "aux", None),
        check_vma=False,
    )
```

```python
import functools

import jax
import jax.numpy as jnp
from jax import lax
from jax.experimental import pallas as pl
from jax.experimental.pallas import tpu as pltpu
from jax.sharding import PartitionSpec as P

BLK = 128
OCC_DEV = 2
PARTNERS = 2
ODB = 9
VB = 8
OFB = 10
FB = 8
LATE = 4
EARLY = ODB - LATE
ROWP = 5
HALF = BLK // 2
F32 = jnp.float32
BF16 = jnp.bfloat16

EARLY_UNITS = (
    [(0, c) for c in range(ODB)]
    + [(1, c) for c in range(ODB)]
    + [(2, c) for c in range(ODB)]
    + [(3, c) for c in range(EARLY)]
)
LATE_UNITS = [(3, c) for c in range(EARLY, ODB)]
EARLY_GROUPS = len(EARLY_UNITS) // 4
VMEM_LIMIT = 60 * 1024 * 1024


def pack_kernel(pick_ref, rows_ref, early_ref, late_ref, spread):
    owners = early_ref.shape[0]
    for o in range(4):
        units = [(n, c) for n, (q, c) in enumerate(EARLY_UNITS + LATE_UNITS) if q == o]
        for w in range(2):
            picked = jnp.dot(
                pick_ref[o * owners : (o + 1) * owners, :],
                rows_ref[w],
                preferred_element_type=F32,
            )
            for n, c in units:
                spread[n // 4, pl.ds((n % 4) * 2 + w, owners, stride=8), :] = picked[
                    :, c * BLK : (c + 1) * BLK
                ]
    for g in range(EARLY_GROUPS):
        early_ref[:, 0, g] = spread[g].reshape(owners, 8, BLK).astype(BF16)
    late_ref[:, 0] = spread[EARLY_GROUPS].reshape(owners, 8, BLK).astype(BF16)


def pack(pick, rows, owners):
    orbitals, width = rows.shape[1], rows.shape[2]
    return pl.pallas_call(
        pack_kernel,
        grid=(ROWP,),
        in_specs=[
            pl.BlockSpec((4 * owners, orbitals), lambda r: (0, 0)),
            pl.BlockSpec((2, orbitals, width), lambda r: (r, 0, 0)),
        ],
        out_specs=[
            pl.BlockSpec((owners, 1, EARLY_GROUPS, 8, BLK), lambda r: (0, r, 0, 0, 0)),
            pl.BlockSpec((owners, 1, 8, BLK), lambda r: (0, r, 0, 0)),
        ],
        out_shape=[
            jax.ShapeDtypeStruct((owners, ROWP, EARLY_GROUPS, 8, BLK), BF16),
            jax.ShapeDtypeStruct((owners, ROWP, 8, BLK), BF16),
        ],
        scratch_shapes=[pltpu.VMEM((EARLY_GROUPS + 1, owners * 8, BLK), F32)],
        compiler_params=pltpu.CompilerParams(vmem_limit_bytes=24 * 1024 * 1024),
        name="pack",
    )(pick, rows)


def sorted_rows(order, block):
    rows = jnp.concatenate(
        [b.astype(F32).reshape(-1, BLK).astype(BF16) for b in block], axis=1
    )
    return jnp.dot(order, rows, preferred_element_type=F32)


def row_energies(energy_ref, p, base):
    parts = [
        energy_ref[p, :, pl.ds(pl.multiple_of(base + i * BLK, BLK), BLK)].reshape(BLK, 1)
        for i in range(VB // 2)
    ]
    return jnp.concatenate(parts, axis=0)


def amplitudes(product, v, p, count_ref, occ_ref, energy_ref, base, row_energy):
    at = pl.multiple_of(v * BLK, BLK)
    live_limit = count_ref[p, 0] * BLK
    denominator = (
        row_energy + energy_ref[p, :, pl.ds(at, BLK)] - occ_ref[0, p] - occ_ref[1, p]
    )
    row = base + lax.broadcasted_iota(jnp.int32, (product.shape[0], 1), 0)
    live = (row < live_limit) & (at < live_limit)
    return jnp.where(live, -product / denominator, 0.0).astype(BF16)


def middle_kernel(
    vir_ref, fit_ref, count_ref, occ_ref, aux_ref, early_ref,
    order_ref, own_ref, other_ref, energy_ref,
    out_ref, left1_ref,
    blocks, first, second, left0,
):
    step = pl.program_id(0)
    pairs = own_ref.shape[0] // 2
    half_blocks = VB // 2
    rows = half_blocks * BLK
    aux = aux_ref[0]
    for h, source in enumerate((own_ref, other_ref)):
        at = pl.multiple_of((h * OFB + step) * BLK, BLK)
        for g in range(0, EARLY_GROUPS, 2):
            halves = [
                sorted_rows(
                    order_ref[...],
                    [source[s * pairs : (s + 1) * pairs, g + i] for i in range(2)],
                )
                for s in range(2)
            ]
            for i in range(2):
                for j in range(4):
                    o, c = EARLY_UNITS[(g + i) * 4 + j]
                    block = jnp.concatenate(
                        [x[j * HALF : (j + 1) * HALF, i * BLK : (i + 1) * BLK] for x in halves],
                        axis=0,
                    ).astype(BF16)
                    if o < 2:
                        blocks[h, o * ODB + c, step] = block.T
                    elif o == 2:
                        first[pl.ds(at, BLK), c * BLK : (c + 1) * BLK] = block
                    else:
                        second[pl.ds(at, BLK), c * BLK : (c + 1) * BLK] = block

    @pl.when(step == pl.num_programs(0) - 1)
    def _():
        for m, left in enumerate((left0, left1_ref)):
            left[...] = jnp.zeros_like(left)
            for k in range(OCC_DEV):
                p = k * PARTNERS + m
                for h in range(2):

                    @pl.loop(0, count_ref[p, 1])
                    def _(f, p=p, k=k, h=h, left=left):
                        left_pos = fit_ref[h, p, 0, f]
                        at = pl.multiple_of((h * OFB + fit_ref[h, p, 1, f]) * BLK, BLK)
                        for v in range(half_blocks):
                            c = vir_ref[p, 0, aux * half_blocks + v]
                            where = slice(k * rows + v * BLK, k * rows + (v + 1) * BLK)
                            left[where, pl.ds(at, BLK)] = blocks[h, k * ODB + c, left_pos]

        for m, (left, right, turns) in enumerate(
            ((left0, first, VB // 2), (left1_ref, second, early_ref.shape[1] // 2))
        ):

            @pl.loop(0, OCC_DEV * turns)
            def _(i, m=m, left=left, right=right, turns=turns):
                k = i // turns
                p = k * PARTNERS + m
                base = aux * rows
                row_energy = row_energies(energy_ref, p, base)
                at = [(i % turns) * 2 + n for n in range(2)]
                if m == 1:
                    at = [early_ref[p, n] for n in at]
                columns = [pl.multiple_of(vir_ref[p, 1, v] * BLK, BLK) for v in at]
                product = jnp.dot(
                    left[pl.ds(pl.multiple_of(k * rows, rows), rows), :],
                    jnp.concatenate([right[:, pl.ds(c, BLK)] for c in columns], axis=1),
                    preferred_element_type=F32,
                )
                for n, v in enumerate(at):
                    out_ref[p, :, pl.ds(pl.multiple_of(v * BLK, BLK), BLK)] = amplitudes(
                        product[:, n * BLK : (n + 1) * BLK],
                        v, p, count_ref, occ_ref, energy_ref, base, row_energy,
                    )


def middle(scalars, order, own, other, energies):
    pairs = own.shape[0]
    depth = 2 * OFB * BLK
    rows = VB // 2 * BLK
    raw = pl.BlockSpec((pairs // OFB, EARLY_GROUPS, 8, BLK), lambda f, *_: (f, 0, 0, 0))
    out = jax.ShapeDtypeStruct((OCC_DEV * PARTNERS, rows, VB * BLK), BF16)
    left1 = jax.ShapeDtypeStruct((OCC_DEV * rows, depth), BF16)
    return pl.pallas_call(
        middle_kernel,
        grid_spec=pltpu.PrefetchScalarGridSpec(
            num_scalar_prefetch=len(scalars),
            grid=(OFB,),
            in_specs=[
                pl.BlockSpec(order.shape, lambda f, *_: (0, 0)),
                raw,
                raw,
                pl.BlockSpec(energies.shape, lambda f, *_: (0, 0, 0)),
            ],
            out_specs=[
                pl.BlockSpec(out.shape, lambda f, *_: (0, 0, 0)),
                pl.BlockSpec(left1.shape, lambda f, *_: (0, 0)),
            ],
            scratch_shapes=[
                pltpu.VMEM((2, OCC_DEV * ODB, OFB, BLK, BLK), BF16),
                pltpu.VMEM((depth, ODB * BLK), BF16),
                pltpu.VMEM((depth, EARLY * BLK), BF16),
                pltpu.VMEM(left1.shape, BF16),
            ],
        ),
        out_shape=[out, left1],
        compiler_params=pltpu.CompilerParams(vmem_limit_bytes=VMEM_LIMIT),
        name="middle",
    )(*scalars, order, own, other, energies)


def late_kernel(
    vir_ref, late_ref, count_ref, occ_ref, aux_ref,
    order_ref, left_ref, own_ref, other_ref, energy_ref, before_ref,
    out_ref, right,
):
    k = pl.program_id(0)
    p = k * PARTNERS + 1
    group = order_ref.shape[0] // 8
    chunks = own_ref.shape[0] // group

    @pl.when(k == 0)
    def _():
        for h, source in enumerate((own_ref, other_ref)):
            for s in range(0, chunks, 4):
                done = sorted_rows(
                    order_ref[...],
                    [source[(s + i) * group : (s + i + 1) * group] for i in range(4)],
                ).astype(BF16)
                for i in range(4):
                    at = (h * chunks + s + i) * HALF
                    for j in range(4):
                        right[at : at + HALF, j * BLK : (j + 1) * BLK] = done[
                            j * HALF : (j + 1) * HALF, i * BLK : (i + 1) * BLK
                        ]

    out_ref[...] = before_ref[...]
    base = aux_ref[0] * left_ref.shape[0]
    row_energy = row_energies(energy_ref, p, base)
    for turn in range(LATE // 2):
        at = [late_ref[p, turn * 2 + n] for n in range(2)]
        columns = [pl.multiple_of((vir_ref[p, 1, v] - EARLY) * BLK, BLK) for v in at]
        product = jnp.dot(
            left_ref[...],
            jnp.concatenate([right[:, pl.ds(c, BLK)] for c in columns], axis=1),
            preferred_element_type=F32,
        )
        for n, v in enumerate(at):
            out_ref[0, :, pl.ds(pl.multiple_of(v * BLK, BLK), BLK)] = amplitudes(
                product[:, n * BLK : (n + 1) * BLK],
                v, p, count_ref, occ_ref, energy_ref, base, row_energy,
            )


def late_products(scalars, order, left1, own, other, energies, before):
    depth = left1.shape[1]
    rows = left1.shape[0] // OCC_DEV
    out = pl.BlockSpec((1, rows, VB * BLK), lambda k, *_: (k * PARTNERS + 1, 0, 0))
    return pl.pallas_call(
        late_kernel,
        grid_spec=pltpu.PrefetchScalarGridSpec(
            num_scalar_prefetch=len(scalars),
            grid=(OCC_DEV,),
            in_specs=[
                pl.BlockSpec(order.shape, lambda k, *_: (0, 0)),
                pl.BlockSpec((rows, depth), lambda k, *_: (k, 0)),
                pl.BlockSpec(own.shape, lambda k, *_: (0, 0, 0)),
                pl.BlockSpec(other.shape, lambda k, *_: (0, 0, 0)),
                pl.BlockSpec(energies.shape, lambda k, *_: (0, 0, 0)),
                out,
            ],
            out_specs=out,
            scratch_shapes=[pltpu.VMEM((depth, LATE * BLK), BF16)],
        ),
        out_shape=jax.ShapeDtypeStruct(before.shape, BF16),
        input_output_aliases={len(scalars) + 5: 0},
        compiler_params=pltpu.CompilerParams(vmem_limit_bytes=32 * 1024 * 1024),
        name="late",
    )(*scalars, order, left1, own, other, energies, before)


def per_device(
    three_index, partners, vir_blocks, fit_blocks, block_counts, virt_energies, occ_energies
):
    owners = lax.axis_size("occ")
    owner = lax.axis_index("occ")
    aux = lax.axis_index("aux").reshape(1)
    pairs_dev = OCC_DEV * PARTNERS

    def swap(x):
        return lax.ppermute(x, "aux", [(0, 1), (1, 0)])

    rows = jnp.transpose(three_index[0], (1, 0, 2))
    orbitals = jnp.arange(rows.shape[1], dtype=jnp.int32)
    wanted = jnp.concatenate(
        [orbitals.reshape(owners, OCC_DEV).T.reshape(-1), partners.reshape(owners, PARTNERS).T.reshape(-1)]
    )
    pick = (wanted[:, None] == orbitals[None, :]).astype(BF16)
    early, late = pack(pick, rows, owners)
    early = lax.all_to_all(early, "occ", 0, 0, tiled=True)
    late = lax.all_to_all(late, "occ", 0, 0, tiled=True)

    fit_own = fit_blocks[:, :, 0, :]
    fits = jnp.stack([fit_own, swap(fit_own)])
    vir = lax.dynamic_slice_in_dim(vir_blocks, owner * pairs_dev, pairs_dev, 0)
    numbers = jnp.arange(VB, dtype=jnp.int32)
    is_late = vir[:, 1, :] >= EARLY

    def listed(flags, length):
        upto = numbers[None, :] <= numbers[:, None]
        rank = jnp.sum(jnp.where(flags[:, None, :] & upto, 1, 0), axis=2)
        total = rank[:, -1:]
        nth = jnp.minimum(jnp.arange(1, length + 1, dtype=jnp.int32), total)
        hit = flags[:, None, :] & (rank[:, None, :] == nth[:, :, None])
        return jnp.sum(jnp.where(hit, numbers, 0), axis=2)

    early_at = listed(~is_late, EARLY + 1)
    late_at = listed(is_late, LATE)
    mine = lax.dynamic_slice_in_dim(occ_energies, owner * OCC_DEV, OCC_DEV, 0)
    partner_ids = lax.dynamic_slice_in_dim(partners, owner * PARTNERS, PARTNERS, 0)
    theirs = jnp.sum(
        jnp.where(partner_ids[:, None] == orbitals[None, :], occ_energies[None, :], 0.0), axis=1
    )
    occ_pair = jnp.stack([jnp.repeat(mine, PARTNERS), jnp.concatenate([theirs] * OCC_DEV)])
    energies = virt_energies[:, None, :]

    place = jnp.arange(256, dtype=jnp.int32)
    source = (place % HALF) // 2 * 8 + (place // HALF) * 2 + place % 2
    order = (source[:, None] == place[None, :]).astype(BF16)

    early = early.reshape(owners * ROWP, EARLY_GROUPS, 8, BLK)
    scalars = (vir, fits, block_counts, occ_pair, aux, early_at)
    out, left1 = middle(scalars, order, early, swap(early), energies)
    late, out = lax.optimization_barrier((late, out))
    late = late.reshape(owners * ROWP, 8, BLK)
    scalars = (vir, late_at, block_counts, occ_pair, aux)
    return late_products(scalars, order, left1, late, swap(late), energies, out)


def solution(mesh):
    return jax.shard_map(
        per_device,
        mesh=mesh,
        in_specs=(
            P("aux", None, "occ", None),
            P(),
            P(),
            P("occ", None, "aux", None),
            P("occ", None),
            P("occ", None),
            P(),
        ),
        out_specs=P("occ", "aux", None),
        check_vma=False,
    )
```

```python
import functools

import jax
import jax.numpy as jnp
from jax import lax
from jax.experimental import pallas as pl
from jax.experimental.pallas import tpu as pltpu
from jax.sharding import PartitionSpec as P

BLK = 128
OCC_DEV = 2
PARTNERS = 2
ODB = 9
VB = 8
OFB = 10
FB = 8
LATE = 4
EARLY = ODB - LATE
ROWP = 5
HALF = BLK // 2
F32 = jnp.float32
BF16 = jnp.bfloat16

EARLY_UNITS = (
    [(0, c) for c in range(ODB)]
    + [(1, c) for c in range(ODB)]
    + [(2, c) for c in range(ODB)]
    + [(3, c) for c in range(EARLY)]
)
LATE_UNITS = [(3, c) for c in range(EARLY, ODB)]
EARLY_GROUPS = len(EARLY_UNITS) // 4


def pack_kernel(pick_ref, rows_ref, early_ref, late_ref, spread):
    owners = early_ref.shape[0]
    for w in range(2):
        picked = jnp.dot(pick_ref[...], rows_ref[w], preferred_element_type=F32)
        for n, (o, c) in enumerate(EARLY_UNITS + LATE_UNITS):
            spread[n // 4, pl.ds((n % 4) * 2 + w, owners, stride=8), :] = picked[
                o * owners : (o + 1) * owners, c * BLK : (c + 1) * BLK
            ]
    for g in range(EARLY_GROUPS):
        early_ref[:, 0, g] = spread[g].reshape(owners, 8, BLK).astype(BF16)
    late_ref[:, 0] = spread[EARLY_GROUPS].reshape(owners, 8, BLK).astype(BF16)


def pack(pick, rows, owners):
    orbitals, width = rows.shape[1], rows.shape[2]
    return pl.pallas_call(
        pack_kernel,
        grid=(ROWP,),
        in_specs=[
            pl.BlockSpec((4 * owners, orbitals), lambda r: (0, 0)),
            pl.BlockSpec((2, orbitals, width), lambda r: (r, 0, 0)),
        ],
        out_specs=[
            pl.BlockSpec((owners, 1, EARLY_GROUPS, 8, BLK), lambda r: (0, r, 0, 0, 0)),
            pl.BlockSpec((owners, 1, 8, BLK), lambda r: (0, r, 0, 0)),
        ],
        out_shape=[
            jax.ShapeDtypeStruct((owners, ROWP, EARLY_GROUPS, 8, BLK), BF16),
            jax.ShapeDtypeStruct((owners, ROWP, 8, BLK), BF16),
        ],
        scratch_shapes=[pltpu.VMEM((EARLY_GROUPS + 1, owners * 8, BLK), F32)],
        compiler_params=pltpu.CompilerParams(vmem_limit_bytes=24 * 1024 * 1024),
        name="pack",
    )(pick, rows)


def sorted_rows(order, block):
    rows = jnp.concatenate(
        [b.astype(F32).reshape(-1, BLK).astype(BF16) for b in block], axis=1
    )
    return jnp.dot(order, rows, preferred_element_type=F32)


def row_energies(energy_ref, p, base, rows):
    parts = [
        energy_ref[p, :, pl.ds(pl.multiple_of(base + i, BLK), BLK)].reshape(BLK, 1)
        for i in range(0, rows, BLK)
    ]
    return jnp.concatenate(parts, axis=0)


def amplitudes(product, v, p, count_ref, occ_ref, energy_ref, base, row_energy):
    at = pl.multiple_of(v * BLK, BLK)
    live_limit = count_ref[p, 0] * BLK
    denominator = (
        row_energy + energy_ref[p, :, pl.ds(at, BLK)] - occ_ref[0, p] - occ_ref[1, p]
    )
    row = base + lax.broadcasted_iota(jnp.int32, (product.shape[0], 1), 0)
    live = (row < live_limit) & (at < live_limit)
    return jnp.where(live, -product / denominator, 0.0).astype(BF16)


def unpacked(order, source):
    pairs = source.shape[0] // 2
    for g in range(0, EARLY_GROUPS, 2):
        halves = [
            sorted_rows(order, [source[s * pairs : (s + 1) * pairs, g + i] for i in range(2)])
            for s in range(2)
        ]
        for i in range(2):
            for j in range(4):
                o, c = EARLY_UNITS[(g + i) * 4 + j]
                yield o, c, jnp.concatenate(
                    [x[j * HALF : (j + 1) * HALF, i * BLK : (i + 1) * BLK] for x in halves],
                    axis=0,
                ).astype(BF16)


def middle_kernel(
    vir_ref, fit_ref, count_ref, occ_ref, aux_ref, early_ref,
    order_ref, own_ref, other_ref, energy_ref,
    out_ref, left1_ref,
    blocks, first, second, left0, left1, sent,
):
    step = pl.program_id(0)
    half_blocks = VB // 2
    rows = half_blocks * BLK
    aux = aux_ref[0]
    copies = [
        pltpu.make_async_copy(
            left1.at[k], left1_ref.at[pl.ds(k * rows, rows)], sent.at[k]
        )
        for k in range(OCC_DEV)
    ]

    @pl.when(step < OFB)
    def _():
        for h, source in enumerate((own_ref, other_ref)):
            at = pl.multiple_of((h * OFB + step) * BLK, BLK)
            for o, c, block in unpacked(order_ref[...], source):
                if o < 2:
                    blocks[h, o * ODB + c, step] = block.T
                elif o == 2:
                    first[pl.ds(at, BLK), c * BLK : (c + 1) * BLK] = block
                else:
                    second[pl.ds(at, BLK), c * BLK : (c + 1) * BLK] = block

    def multiply(m, k, left, right, turns):
        p = k * PARTNERS + m
        left[...] = jnp.zeros_like(left)
        for h in range(2):

            @pl.loop(0, count_ref[p, 1])
            def _(f):
                left_pos = fit_ref[h, p, 0, f]
                at = pl.multiple_of((h * OFB + fit_ref[h, p, 1, f]) * BLK, BLK)
                for v in range(half_blocks):
                    c = vir_ref[p, 0, aux * half_blocks + v]
                    left[v * BLK : (v + 1) * BLK, pl.ds(at, BLK)] = blocks[
                        h, k * ODB + c, left_pos
                    ]

        if m == 1:
            copies[k].start()
        base = aux * rows
        row_energy = row_energies(energy_ref, p, base, rows)
        out_ref[...] = jnp.zeros_like(out_ref)
        live_count = count_ref[p, 0]
        live_turns = jnp.int32(0)
        for i in range(turns):
            leading = early_ref[p, i * 2] if m == 1 else i * 2
            live_turns += (leading < live_count).astype(jnp.int32)

        @pl.loop(0, jnp.where(aux * half_blocks < live_count, live_turns, 0))
        def _(i):
            at = [i * 2 + n for n in range(2)]
            if m == 1:
                at = [early_ref[p, n] for n in at]
            columns = [pl.multiple_of(vir_ref[p, 1, v] * BLK, BLK) for v in at]
            product = jnp.dot(
                left[...],
                jnp.concatenate([right[:, pl.ds(c, BLK)] for c in columns], axis=1),
                preferred_element_type=F32,
            )
            for n, v in enumerate(at):
                out_ref[0, :, pl.ds(pl.multiple_of(v * BLK, BLK), BLK)] = amplitudes(
                    product[:, n * BLK : (n + 1) * BLK],
                    v, p, count_ref, occ_ref, energy_ref, base, row_energy,
                )

    for k in range(OCC_DEV):

        @pl.when(step == OFB + k)
        def _(k=k):
            multiply(1, k, left1.at[k], second, early_ref.shape[1] // 2)

        @pl.when(step == OFB + OCC_DEV + k)
        def _(k=k):
            multiply(0, k, left0, first, VB // 2)
            if k == OCC_DEV - 1:
                for copy in copies:
                    copy.wait()


def middle(scalars, order, own, other, energies):
    pairs = other.shape[0]
    depth = 2 * OFB * BLK
    rows = VB // 2 * BLK
    raw = pl.BlockSpec(
        (pairs // OFB, EARLY_GROUPS, 8, BLK),
        lambda f, *_: (jnp.minimum(f, OFB - 1), 0, 0, 0),
    )

    def out_block(f, *_):
        turn = jnp.maximum(f - OFB, 0)
        return (lax.rem(turn, OCC_DEV) * PARTNERS + 1 - turn // OCC_DEV, 0, 0)

    return pl.pallas_call(
        middle_kernel,
        grid_spec=pltpu.PrefetchScalarGridSpec(
            num_scalar_prefetch=len(scalars),
            grid=(OFB + OCC_DEV * PARTNERS,),
            in_specs=[
                pl.BlockSpec(order.shape, lambda f, *_: (0, 0)),
                raw,
                raw,
                pl.BlockSpec(energies.shape, lambda f, *_: (0, 0, 0)),
            ],
            out_specs=[
                pl.BlockSpec((1, rows, VB * BLK), out_block),
                pl.BlockSpec(memory_space=pl.ANY),
            ],
            scratch_shapes=[
                pltpu.VMEM((2, OCC_DEV * ODB, OFB, BLK, BLK), BF16),
                pltpu.VMEM((depth, ODB * BLK), BF16),
                pltpu.VMEM((depth, EARLY * BLK), BF16),
                pltpu.VMEM((rows, depth), BF16),
                pltpu.VMEM((OCC_DEV, rows, depth), BF16),
                pltpu.SemaphoreType.DMA((OCC_DEV,)),
            ],
        ),
        out_shape=[
            jax.ShapeDtypeStruct((OCC_DEV * PARTNERS, rows, VB * BLK), BF16),
            jax.ShapeDtypeStruct((OCC_DEV * rows, depth), BF16),
        ],
        compiler_params=pltpu.CompilerParams(vmem_limit_bytes=60 * 1024 * 1024),
        name="middle",
    )(*scalars, order, own, other, energies)


def late_kernel(
    vir_ref, late_ref, count_ref, occ_ref, aux_ref,
    order_ref, left_ref, own_ref, other_ref, energy_ref, before_ref,
    out_ref, right,
):
    k = pl.program_id(0)
    p = k * PARTNERS + 1
    group = order_ref.shape[0] // 8
    chunks = own_ref.shape[0] // group

    @pl.when(k == 0)
    def _():
        for h, source in enumerate((own_ref, other_ref)):
            for s in range(0, chunks, 4):
                done = sorted_rows(
                    order_ref[...],
                    [source[(s + i) * group : (s + i + 1) * group] for i in range(4)],
                ).astype(BF16)
                for i in range(4):
                    at = (h * chunks + s + i) * HALF
                    for j in range(4):
                        right[at : at + HALF, j * BLK : (j + 1) * BLK] = done[
                            j * HALF : (j + 1) * HALF, i * BLK : (i + 1) * BLK
                        ]

    out_ref[...] = before_ref[...]
    base = aux_ref[0] * left_ref.shape[0]
    row_energy = row_energies(energy_ref, p, base, left_ref.shape[0])
    live_count = count_ref[p, 0]
    for turn in range(LATE // 2):
        leading = late_ref[p, turn * 2]

        @pl.when((leading < live_count) & (aux_ref[0] * (VB // 2) < live_count))
        def _(turn=turn):
            at = [late_ref[p, turn * 2 + n] for n in range(2)]
            columns = [
                pl.multiple_of((vir_ref[p, 1, v] - EARLY) * BLK, BLK) for v in at
            ]
            product = jnp.dot(
                left_ref[...],
                jnp.concatenate([right[:, pl.ds(c, BLK)] for c in columns], axis=1),
                preferred_element_type=F32,
            )
            for n, v in enumerate(at):
                out_ref[0, :, pl.ds(pl.multiple_of(v * BLK, BLK), BLK)] = amplitudes(
                    product[:, n * BLK : (n + 1) * BLK],
                    v, p, count_ref, occ_ref, energy_ref, base, row_energy,
                )


def late_products(scalars, order, left1, own, other, energies, before):
    depth = left1.shape[1]
    rows = left1.shape[0] // OCC_DEV
    out = pl.BlockSpec((1, rows, VB * BLK), lambda k, *_: (k * PARTNERS + 1, 0, 0))
    return pl.pallas_call(
        late_kernel,
        grid_spec=pltpu.PrefetchScalarGridSpec(
            num_scalar_prefetch=len(scalars),
            grid=(OCC_DEV,),
            in_specs=[
                pl.BlockSpec(order.shape, lambda k, *_: (0, 0)),
                pl.BlockSpec((rows, depth), lambda k, *_: (k, 0)),
                pl.BlockSpec(own.shape, lambda k, *_: (0, 0, 0)),
                pl.BlockSpec(other.shape, lambda k, *_: (0, 0, 0)),
                pl.BlockSpec(energies.shape, lambda k, *_: (0, 0, 0)),
                out,
            ],
            out_specs=out,
            scratch_shapes=[pltpu.VMEM((depth, LATE * BLK), BF16)],
        ),
        out_shape=jax.ShapeDtypeStruct(before.shape, BF16),
        input_output_aliases={len(scalars) + 5: 0},
        compiler_params=pltpu.CompilerParams(vmem_limit_bytes=32 * 1024 * 1024),
        name="late",
    )(*scalars, order, left1, own, other, energies, before)


def per_device(
    three_index, partners, vir_blocks, fit_blocks, block_counts, virt_energies, occ_energies
):
    owners = lax.axis_size("occ")
    owner = lax.axis_index("occ")
    aux = lax.axis_index("aux").reshape(1)
    pairs_dev = OCC_DEV * PARTNERS

    def swap(x):
        return lax.ppermute(x, "aux", [(0, 1), (1, 0)])

    rows = jnp.transpose(three_index[0], (1, 0, 2))
    orbitals = jnp.arange(rows.shape[1], dtype=jnp.int32)
    wanted = jnp.concatenate(
        [orbitals.reshape(owners, OCC_DEV).T.reshape(-1), partners.reshape(owners, PARTNERS).T.reshape(-1)]
    )
    pick = (wanted[:, None] == orbitals[None, :]).astype(BF16)
    early, late = pack(pick, rows, owners)
    early = lax.all_to_all(early, "occ", 0, 0, tiled=True)
    late = lax.all_to_all(late, "occ", 0, 0, tiled=True)

    fit_own = fit_blocks[:, :, 0, :]
    fits = jnp.stack([fit_own, swap(fit_own)])
    vir = lax.dynamic_slice_in_dim(vir_blocks, owner * pairs_dev, pairs_dev, 0)
    numbers = jnp.arange(VB, dtype=jnp.int32)
    is_late = vir[:, 1, :] >= EARLY

    def listed(flags, length):
        upto = numbers[None, :] <= numbers[:, None]
        rank = jnp.sum(jnp.where(flags[:, None, :] & upto, 1, 0), axis=2)
        total = rank[:, -1:]
        index = jnp.arange(1, length + 1, dtype=jnp.int32)
        nth = jnp.minimum(index, total)
        hit = flags[:, None, :] & (rank[:, None, :] == nth[:, :, None])
        found = jnp.sum(jnp.where(hit, numbers, 0), axis=2)
        return jnp.where(index <= total + total % 2, found, VB)

    early_at = listed(~is_late, EARLY + 1)
    late_at = listed(is_late, LATE)
    mine = lax.dynamic_slice_in_dim(occ_energies, owner * OCC_DEV, OCC_DEV, 0)
    partner_ids = lax.dynamic_slice_in_dim(partners, owner * PARTNERS, PARTNERS, 0)
    theirs = jnp.sum(
        jnp.where(partner_ids[:, None] == orbitals[None, :], occ_energies[None, :], 0.0), axis=1
    )
    occ_pair = jnp.stack([jnp.repeat(mine, PARTNERS), jnp.concatenate([theirs] * OCC_DEV)])
    energies = virt_energies[:, None, :]

    place = jnp.arange(256, dtype=jnp.int32)
    source = (place % HALF) // 2 * 8 + (place // HALF) * 2 + place % 2
    order = (source[:, None] == place[None, :]).astype(BF16)

    early = early.reshape(owners * ROWP, EARLY_GROUPS, 8, BLK)
    scalars = (vir, fits, block_counts, occ_pair, aux, early_at)
    out, left1 = middle(scalars, order, early, swap(early), energies)
    late, out = lax.optimization_barrier((late, out))
    late = late.reshape(owners * ROWP, 8, BLK)
    scalars = (vir, late_at, block_counts, occ_pair, aux)
    return late_products(scalars, order, left1, late, swap(late), energies, out)


def solution(mesh):
    return jax.shard_map(
        per_device,
        mesh=mesh,
        in_specs=(
            P("aux", None, "occ", None),
            P(),
            P(),
            P("occ", None, "aux", None),
            P("occ", None),
            P("occ", None),
            P(),
        ),
        out_specs=P("occ", "aux", None),
        check_vma=False,
    )
```

```python
import functools

import jax
import jax.numpy as jnp
from jax import lax
from jax.experimental import pallas as pl
from jax.experimental.pallas import tpu as pltpu
from jax.sharding import PartitionSpec as P

BLK = 128
OCC_DEV = 2
PARTNERS = 2
ODB = 9
VB = 8
OFB = 10
FB = 8
LATE = 4
EARLY = ODB - LATE
ROWP = 5
HALF = BLK // 2
F32 = jnp.float32
BF16 = jnp.bfloat16

EARLY_UNITS = (
    [(0, c) for c in range(ODB)]
    + [(1, c) for c in range(ODB)]
    + [(2, c) for c in range(ODB)]
    + [(3, c) for c in range(EARLY)]
)
LATE_UNITS = [(3, c) for c in range(EARLY, ODB)]
EARLY_GROUPS = len(EARLY_UNITS) // 4


def pack_kernel(pick_ref, rows_ref, early_ref, late_ref, spread):
    owners = early_ref.shape[0]
    for w in range(2):
        picked = jnp.dot(pick_ref[...], rows_ref[w], preferred_element_type=F32)
        for n, (o, c) in enumerate(EARLY_UNITS + LATE_UNITS):
            spread[n // 4, pl.ds((n % 4) * 2 + w, owners, stride=8), :] = picked[
                o * owners : (o + 1) * owners, c * BLK : (c + 1) * BLK
            ]
    for g in range(EARLY_GROUPS):
        early_ref[:, 0, g] = spread[g].reshape(owners, 8, BLK).astype(BF16)
    late_ref[:, 0] = spread[EARLY_GROUPS].reshape(owners, 8, BLK).astype(BF16)


def pack(pick, rows, owners):
    orbitals, width = rows.shape[1], rows.shape[2]
    return pl.pallas_call(
        pack_kernel,
        grid=(ROWP,),
        in_specs=[
            pl.BlockSpec((4 * owners, orbitals), lambda r: (0, 0)),
            pl.BlockSpec((2, orbitals, width), lambda r: (r, 0, 0)),
        ],
        out_specs=[
            pl.BlockSpec((owners, 1, EARLY_GROUPS, 8, BLK), lambda r: (0, r, 0, 0, 0)),
            pl.BlockSpec((owners, 1, 8, BLK), lambda r: (0, r, 0, 0)),
        ],
        out_shape=[
            jax.ShapeDtypeStruct((owners, ROWP, EARLY_GROUPS, 8, BLK), BF16),
            jax.ShapeDtypeStruct((owners, ROWP, 8, BLK), BF16),
        ],
        scratch_shapes=[pltpu.VMEM((EARLY_GROUPS + 1, owners * 8, BLK), F32)],
        compiler_params=pltpu.CompilerParams(vmem_limit_bytes=24 * 1024 * 1024),
        name="pack",
    )(pick, rows)


def sorted_rows(order, block):
    rows = jnp.concatenate(
        [b.astype(F32).reshape(-1, BLK).astype(BF16) for b in block], axis=1
    )
    return jnp.dot(order, rows, preferred_element_type=F32)


def row_energies(energy_ref, p, base, rows):
    parts = [
        energy_ref[p, :, pl.ds(pl.multiple_of(base + i, BLK), BLK)].reshape(BLK, 1)
        for i in range(0, rows, BLK)
    ]
    return jnp.concatenate(parts, axis=0)


def amplitudes(product, v, p, count_ref, occ_ref, energy_ref, base, row_energy):
    at = pl.multiple_of(v * BLK, BLK)
    live_limit = count_ref[p, 0] * BLK
    denominator = (
        row_energy + energy_ref[p, :, pl.ds(at, BLK)] - occ_ref[0, p] - occ_ref[1, p]
    )
    row = base + lax.broadcasted_iota(jnp.int32, (product.shape[0], 1), 0)
    live = (row < live_limit) & (at < live_limit)
    return jnp.where(live, -product / denominator, 0.0).astype(BF16)


def unpacked(order, source):
    pairs = source.shape[0] // 2
    for g in range(0, EARLY_GROUPS, 2):
        halves = [
            sorted_rows(order, [source[s * pairs : (s + 1) * pairs, g + i] for i in range(2)])
            for s in range(2)
        ]
        for i in range(2):
            for j in range(4):
                o, c = EARLY_UNITS[(g + i) * 4 + j]
                yield o, c, jnp.concatenate(
                    [x[j * HALF : (j + 1) * HALF, i * BLK : (i + 1) * BLK] for x in halves],
                    axis=0,
                ).astype(BF16)


def middle_kernel(
    vir_ref, fit_ref, count_ref, occ_ref, aux_ref, early_ref,
    order_ref, own_ref, other_ref, energy_ref,
    out_ref, left1_ref,
    blocks, first, second, left0, left1, sent,
):
    step = pl.program_id(0)
    half_blocks = VB // 2
    rows = half_blocks * BLK
    aux = aux_ref[0]
    copies = [
        pltpu.make_async_copy(
            left1.at[k], left1_ref.at[pl.ds(k * rows, rows)], sent.at[k]
        )
        for k in range(OCC_DEV)
    ]

    @pl.when(step < OFB)
    def _():
        for h, source in enumerate((own_ref, other_ref)):
            at = pl.multiple_of((h * OFB + step) * BLK, BLK)
            for o, c, block in unpacked(order_ref[...], source):
                if o < 2:
                    blocks[h, o * ODB + c, step] = block.T
                elif o == 2:
                    first[pl.ds(at, BLK), c * BLK : (c + 1) * BLK] = block
                else:
                    second[pl.ds(at, BLK), c * BLK : (c + 1) * BLK] = block

    def multiply(m, k, left, right, turns):
        p = k * PARTNERS + m
        left[...] = jnp.zeros_like(left)
        for h in range(2):

            @pl.loop(0, count_ref[p, 1])
            def _(f):
                left_pos = fit_ref[h, p, 0, f]
                at = pl.multiple_of((h * OFB + fit_ref[h, p, 1, f]) * BLK, BLK)
                for v in range(half_blocks):
                    c = vir_ref[p, 0, aux * half_blocks + v]
                    left[v * BLK : (v + 1) * BLK, pl.ds(at, BLK)] = blocks[
                        h, k * ODB + c, left_pos
                    ]

        if m == 1:
            copies[k].start()
        base = aux * rows
        row_energy = row_energies(energy_ref, p, base, rows)
        out_ref[...] = jnp.zeros_like(out_ref)
        live_count = count_ref[p, 0]
        live_turns = jnp.int32(0)
        for i in range(turns):
            leading = early_ref[p, i * 2] if m == 1 else i * 2
            live_turns += (leading < live_count).astype(jnp.int32)

        @pl.loop(0, jnp.where(aux * half_blocks < live_count, live_turns, 0))
        def _(i):
            at = [i * 2 + n for n in range(2)]
            if m == 1:
                at = [early_ref[p, n] for n in at]
            columns = [pl.multiple_of(vir_ref[p, 1, v] * BLK, BLK) for v in at]
            product = jnp.dot(
                left[...],
                jnp.concatenate([right[:, pl.ds(c, BLK)] for c in columns], axis=1),
                preferred_element_type=F32,
            )
            for n, v in enumerate(at):
                out_ref[0, :, pl.ds(pl.multiple_of(v * BLK, BLK), BLK)] = amplitudes(
                    product[:, n * BLK : (n + 1) * BLK],
                    v, p, count_ref, occ_ref, energy_ref, base, row_energy,
                )

    for k in range(OCC_DEV):

        @pl.when(step == OFB + k)
        def _(k=k):
            multiply(1, k, left1.at[k], second, early_ref.shape[1] // 2)

        @pl.when(step == OFB + OCC_DEV + k)
        def _(k=k):
            multiply(0, k, left0, first, VB // 2)
            if k == OCC_DEV - 1:
                for copy in copies:
                    copy.wait()


def middle(scalars, order, own, other, energies):
    pairs = other.shape[0]
    depth = 2 * OFB * BLK
    rows = VB // 2 * BLK
    raw = pl.BlockSpec(
        (pairs // OFB, EARLY_GROUPS, 8, BLK),
        lambda f, *_: (jnp.minimum(f, OFB - 1), 0, 0, 0),
    )

    def out_block(f, *_):
        turn = jnp.maximum(f - OFB, 0)
        return (lax.rem(turn, OCC_DEV) * PARTNERS + 1 - turn // OCC_DEV, 0, 0)

    return pl.pallas_call(
        middle_kernel,
        grid_spec=pltpu.PrefetchScalarGridSpec(
            num_scalar_prefetch=len(scalars),
            grid=(OFB + OCC_DEV * PARTNERS,),
            in_specs=[
                pl.BlockSpec(order.shape, lambda f, *_: (0, 0)),
                raw,
                raw,
                pl.BlockSpec(energies.shape, lambda f, *_: (0, 0, 0)),
            ],
            out_specs=[
                pl.BlockSpec((1, rows, VB * BLK), out_block),
                pl.BlockSpec(memory_space=pl.ANY),
            ],
            scratch_shapes=[
                pltpu.VMEM((2, OCC_DEV * ODB, OFB, BLK, BLK), BF16),
                pltpu.VMEM((depth, ODB * BLK), BF16),
                pltpu.VMEM((depth, EARLY * BLK), BF16),
                pltpu.VMEM((rows, depth), BF16),
                pltpu.VMEM((OCC_DEV, rows, depth), BF16),
                pltpu.SemaphoreType.DMA((OCC_DEV,)),
            ],
        ),
        out_shape=[
            jax.ShapeDtypeStruct((OCC_DEV * PARTNERS, rows, VB * BLK), BF16),
            jax.ShapeDtypeStruct((OCC_DEV * rows, depth), BF16),
        ],
        compiler_params=pltpu.CompilerParams(vmem_limit_bytes=60 * 1024 * 1024),
        name="middle",
    )(*scalars, order, own, other, energies)


def stage_kernel(from_ref, to_ref, done):
    copies = [
        pltpu.make_async_copy(from_ref.at[part], to_ref.at[part], done.at[n])
        for n, part in enumerate(
            pl.ds(n * from_ref.shape[0] // 4, from_ref.shape[0] // 4) for n in range(4)
        )
    ]
    for copy in copies:
        copy.start()
    for copy in copies:
        copy.wait()


def stage(x):
    return pl.pallas_call(
        stage_kernel,
        in_specs=[pl.BlockSpec(memory_space=pl.ANY)],
        out_specs=pl.BlockSpec(memory_space=pl.ANY),
        out_shape=jax.ShapeDtypeStruct(x.shape, x.dtype),
        scratch_shapes=[pltpu.SemaphoreType.DMA((4,))],
        compiler_params=pltpu.CompilerParams(vmem_limit_bytes=1024 * 1024),
        name="stage",
    )(x)


def late_kernel(
    vir_ref, late_ref, count_ref, occ_ref, aux_ref,
    order_ref, left_ref, own_ref, other_ref, energy_ref, before_ref,
    out_ref, right,
):
    k = pl.program_id(0)
    p = k * PARTNERS + 1
    group = order_ref.shape[0] // 8
    chunks = own_ref.shape[0] // group

    @pl.when(k == 0)
    def _():
        for h, source in enumerate((own_ref, other_ref)):
            for s in range(0, chunks, 4):
                done = sorted_rows(
                    order_ref[...],
                    [source[(s + i) * group : (s + i + 1) * group] for i in range(4)],
                ).astype(BF16)
                for i in range(4):
                    at = (h * chunks + s + i) * HALF
                    for j in range(4):
                        right[at : at + HALF, j * BLK : (j + 1) * BLK] = done[
                            j * HALF : (j + 1) * HALF, i * BLK : (i + 1) * BLK
                        ]

    out_ref[...] = before_ref[...]
    base = aux_ref[0] * left_ref.shape[0]
    row_energy = row_energies(energy_ref, p, base, left_ref.shape[0])
    live_count = count_ref[p, 0]
    for turn in range(LATE // 2):
        leading = late_ref[p, turn * 2]

        @pl.when((leading < live_count) & (aux_ref[0] * (VB // 2) < live_count))
        def _(turn=turn):
            at = [late_ref[p, turn * 2 + n] for n in range(2)]
            columns = [
                pl.multiple_of((vir_ref[p, 1, v] - EARLY) * BLK, BLK) for v in at
            ]
            product = jnp.dot(
                left_ref[...],
                jnp.concatenate([right[:, pl.ds(c, BLK)] for c in columns], axis=1),
                preferred_element_type=F32,
            )
            for n, v in enumerate(at):
                out_ref[0, :, pl.ds(pl.multiple_of(v * BLK, BLK), BLK)] = amplitudes(
                    product[:, n * BLK : (n + 1) * BLK],
                    v, p, count_ref, occ_ref, energy_ref, base, row_energy,
                )


def late_products(scalars, order, left1, own, other, energies, before):
    depth = left1.shape[1]
    rows = left1.shape[0] // OCC_DEV
    out = pl.BlockSpec((1, rows, VB * BLK), lambda k, *_: (k * PARTNERS + 1, 0, 0))
    return pl.pallas_call(
        late_kernel,
        grid_spec=pltpu.PrefetchScalarGridSpec(
            num_scalar_prefetch=len(scalars),
            grid=(OCC_DEV,),
            in_specs=[
                pl.BlockSpec(order.shape, lambda k, *_: (0, 0)),
                pl.BlockSpec((rows, depth), lambda k, *_: (k, 0)),
                pl.BlockSpec(own.shape, lambda k, *_: (0, 0, 0)),
                pl.BlockSpec(other.shape, lambda k, *_: (0, 0, 0)),
                pl.BlockSpec(energies.shape, lambda k, *_: (0, 0, 0)),
                out,
            ],
            out_specs=out,
            scratch_shapes=[pltpu.VMEM((depth, LATE * BLK), BF16)],
        ),
        out_shape=jax.ShapeDtypeStruct(before.shape, BF16),
        input_output_aliases={len(scalars) + 5: 0},
        compiler_params=pltpu.CompilerParams(vmem_limit_bytes=32 * 1024 * 1024),
        name="late",
    )(*scalars, order, left1, own, other, energies, before)


def per_device(
    three_index, partners, vir_blocks, fit_blocks, block_counts, virt_energies, occ_energies
):
    owners = lax.axis_size("occ")
    owner = lax.axis_index("occ")
    aux = lax.axis_index("aux").reshape(1)
    pairs_dev = OCC_DEV * PARTNERS

    def swap(x):
        return lax.ppermute(x, "aux", [(0, 1), (1, 0)])

    rows = jnp.transpose(three_index[0], (1, 0, 2))
    orbitals = jnp.arange(rows.shape[1], dtype=jnp.int32)
    wanted = jnp.concatenate(
        [orbitals.reshape(owners, OCC_DEV).T.reshape(-1), partners.reshape(owners, PARTNERS).T.reshape(-1)]
    )
    pick = (wanted[:, None] == orbitals[None, :]).astype(BF16)
    early, late = pack(pick, rows, owners)
    early = lax.all_to_all(early, "occ", 0, 0, tiled=True)
    late = lax.all_to_all(late, "occ", 0, 0, tiled=True)

    fit_own = fit_blocks[:, :, 0, :]
    fits = jnp.stack([fit_own, swap(fit_own)])
    vir = lax.dynamic_slice_in_dim(vir_blocks, owner * pairs_dev, pairs_dev, 0)
    numbers = jnp.arange(VB, dtype=jnp.int32)
    is_late = vir[:, 1, :] >= EARLY

    def listed(flags, length):
        upto = numbers[None, :] <= numbers[:, None]
        rank = jnp.sum(jnp.where(flags[:, None, :] & upto, 1, 0), axis=2)
        total = rank[:, -1:]
        index = jnp.arange(1, length + 1, dtype=jnp.int32)
        nth = jnp.minimum(index, total)
        hit = flags[:, None, :] & (rank[:, None, :] == nth[:, :, None])
        found = jnp.sum(jnp.where(hit, numbers, 0), axis=2)
        return jnp.where(index <= total + total % 2, found, VB)

    early_at = listed(~is_late, EARLY + 1)
    late_at = listed(is_late, LATE)
    mine = lax.dynamic_slice_in_dim(occ_energies, owner * OCC_DEV, OCC_DEV, 0)
    partner_ids = lax.dynamic_slice_in_dim(partners, owner * PARTNERS, PARTNERS, 0)
    theirs = jnp.sum(
        jnp.where(partner_ids[:, None] == orbitals[None, :], occ_energies[None, :], 0.0), axis=1
    )
    occ_pair = jnp.stack([jnp.repeat(mine, PARTNERS), jnp.concatenate([theirs] * OCC_DEV)])
    energies = virt_energies[:, None, :]

    place = jnp.arange(256, dtype=jnp.int32)
    source = (place % HALF) // 2 * 8 + (place // HALF) * 2 + place % 2
    order = (source[:, None] == place[None, :]).astype(BF16)

    early = early.reshape(owners * ROWP, EARLY_GROUPS, 8, BLK)
    scalars = (vir, fits, block_counts, occ_pair, aux, early_at)
    out, left1 = middle(scalars, order, early, swap(early), energies)
    late, out = lax.optimization_barrier((late, out))
    late = late.reshape(owners * ROWP, 8, BLK)
    scalars = (vir, late_at, block_counts, occ_pair, aux)
    return late_products(scalars, order, stage(left1), late, swap(late), energies, out)


def solution(mesh):
    return jax.shard_map(
        per_device,
        mesh=mesh,
        in_specs=(
            P("aux", None, "occ", None),
            P(),
            P(),
            P("occ", None, "aux", None),
            P("occ", None),
            P("occ", None),
            P(),
        ),
        out_specs=P("occ", "aux", None),
        check_vma=False,
    )
```

```python
import functools

import jax
import jax.numpy as jnp
from jax import lax
from jax.experimental import pallas as pl
from jax.experimental.pallas import tpu as pltpu
from jax.sharding import PartitionSpec as P

BLK = 128
OCC_DEV = 2
PARTNERS = 2
ODB = 9
VB = 8
OFB = 10
FB = 8
LATE = 4
EARLY = ODB - LATE
ROWP = 5
HALF = BLK // 2
F32 = jnp.float32
BF16 = jnp.bfloat16

EARLY_UNITS = (
    [(0, c) for c in range(ODB)]
    + [(1, c) for c in range(ODB)]
    + [(2, c) for c in range(ODB)]
    + [(3, c) for c in range(EARLY)]
)
LATE_UNITS = [(3, c) for c in range(EARLY, ODB)]
EARLY_GROUPS = len(EARLY_UNITS) // 4


def pack_kernel(pick_ref, rows_ref, early_ref, late_ref, spread):
    owners = early_ref.shape[0]
    for w in range(2):
        picked = jnp.dot(pick_ref[...], rows_ref[w], preferred_element_type=F32)
        for n, (o, c) in enumerate(EARLY_UNITS + LATE_UNITS):
            spread[n // 4, pl.ds((n % 4) * 2 + w, owners, stride=8), :] = picked[
                o * owners : (o + 1) * owners, c * BLK : (c + 1) * BLK
            ]
    for g in range(EARLY_GROUPS):
        early_ref[:, 0, g] = spread[g].reshape(owners, 8, BLK).astype(BF16)
    late_ref[:, 0] = spread[EARLY_GROUPS].reshape(owners, 8, BLK).astype(BF16)


def pack(pick, rows, owners):
    orbitals, width = rows.shape[1], rows.shape[2]
    return pl.pallas_call(
        pack_kernel,
        grid=(ROWP,),
        in_specs=[
            pl.BlockSpec((4 * owners, orbitals), lambda r: (0, 0)),
            pl.BlockSpec((2, orbitals, width), lambda r: (r, 0, 0)),
        ],
        out_specs=[
            pl.BlockSpec((owners, 1, EARLY_GROUPS, 8, BLK), lambda r: (0, r, 0, 0, 0)),
            pl.BlockSpec((owners, 1, 8, BLK), lambda r: (0, r, 0, 0)),
        ],
        out_shape=[
            jax.ShapeDtypeStruct((owners, ROWP, EARLY_GROUPS, 8, BLK), BF16),
            jax.ShapeDtypeStruct((owners, ROWP, 8, BLK), BF16),
        ],
        scratch_shapes=[pltpu.VMEM((EARLY_GROUPS + 1, owners * 8, BLK), F32)],
        compiler_params=pltpu.CompilerParams(vmem_limit_bytes=24 * 1024 * 1024),
        name="pack",
    )(pick, rows)


def sorted_rows(order, block):
    rows = jnp.concatenate(
        [b.astype(F32).reshape(-1, BLK).astype(BF16) for b in block], axis=1
    )
    return jnp.dot(order, rows, preferred_element_type=F32)


def row_energies(energy_ref, p, base, rows):
    parts = [
        energy_ref[p, :, pl.ds(pl.multiple_of(base + i, BLK), BLK)].reshape(BLK, 1)
        for i in range(0, rows, BLK)
    ]
    return jnp.concatenate(parts, axis=0)


def amplitudes(product, v, p, count_ref, occ_ref, energy_ref, base, row_energy):
    at = pl.multiple_of(v * BLK, BLK)
    live_limit = count_ref[p, 0] * BLK
    denominator = (
        row_energy + energy_ref[p, :, pl.ds(at, BLK)] - occ_ref[0, p] - occ_ref[1, p]
    )
    row = base + lax.broadcasted_iota(jnp.int32, (product.shape[0], 1), 0)
    live = (row < live_limit) & (at < live_limit)
    return jnp.where(live, -product / denominator, 0.0).astype(BF16)


def unpacked(order, source):
    pairs = source.shape[0] // 2
    for g in range(0, EARLY_GROUPS, 2):
        halves = [
            sorted_rows(order, [source[s * pairs : (s + 1) * pairs, g + i] for i in range(2)])
            for s in range(2)
        ]
        for i in range(2):
            for j in range(4):
                o, c = EARLY_UNITS[(g + i) * 4 + j]
                yield o, c, jnp.concatenate(
                    [x[j * HALF : (j + 1) * HALF, i * BLK : (i + 1) * BLK] for x in halves],
                    axis=0,
                ).astype(BF16)


def middle_kernel(
    vir_ref, fit_ref, count_ref, occ_ref, aux_ref, early_ref,
    order_ref, own_ref, other_ref, energy_ref,
    out_ref, left1_ref,
    blocks, first, second, left0, left1, sent,
):
    step = pl.program_id(0)
    half_blocks = VB // 2
    rows = half_blocks * BLK
    aux = aux_ref[0]
    copies = [
        pltpu.make_async_copy(
            left1.at[k], left1_ref.at[pl.ds(k * rows, rows)], sent.at[k]
        )
        for k in range(OCC_DEV)
    ]

    @pl.when(step < OFB)
    def _():
        for h, source in enumerate((own_ref, other_ref)):
            at = pl.multiple_of((h * OFB + step) * BLK, BLK)
            for o, c, block in unpacked(order_ref[...], source):
                if o < 2:
                    blocks[h, o * ODB + c, step] = block.T
                elif o == 2:
                    first[pl.ds(at, BLK), c * BLK : (c + 1) * BLK] = block
                else:
                    second[pl.ds(at, BLK), c * BLK : (c + 1) * BLK] = block

    def multiply(m, k, left, right, turns):
        p = k * PARTNERS + m
        left[...] = jnp.zeros_like(left)
        for h in range(2):

            @pl.loop(0, count_ref[p, 1])
            def _(f):
                left_pos = fit_ref[h, p, 0, f]
                at = pl.multiple_of((h * OFB + fit_ref[h, p, 1, f]) * BLK, BLK)
                for v in range(half_blocks):
                    c = vir_ref[p, 0, aux * half_blocks + v]
                    left[v * BLK : (v + 1) * BLK, pl.ds(at, BLK)] = blocks[
                        h, k * ODB + c, left_pos
                    ]

        if m == 1:
            copies[k].start()
        base = aux * rows
        row_energy = row_energies(energy_ref, p, base, rows)
        out_ref[...] = jnp.zeros_like(out_ref)
        live_count = count_ref[p, 0]
        live_turns = jnp.int32(0)
        for i in range(turns):
            leading = early_ref[p, i * 2] if m == 1 else i * 2
            live_turns += (leading < live_count).astype(jnp.int32)

        @pl.loop(0, jnp.where(aux * half_blocks < live_count, live_turns, 0))
        def _(i):
            at = [i * 2 + n for n in range(2)]
            if m == 1:
                at = [early_ref[p, n] for n in at]
            columns = [pl.multiple_of(vir_ref[p, 1, v] * BLK, BLK) for v in at]
            product = jnp.dot(
                left[...],
                jnp.concatenate([right[:, pl.ds(c, BLK)] for c in columns], axis=1),
                preferred_element_type=F32,
            )
            for n, v in enumerate(at):
                out_ref[0, :, pl.ds(pl.multiple_of(v * BLK, BLK), BLK)] = amplitudes(
                    product[:, n * BLK : (n + 1) * BLK],
                    v, p, count_ref, occ_ref, energy_ref, base, row_energy,
                )

    for k in range(OCC_DEV):

        @pl.when(step == OFB + k)
        def _(k=k):
            multiply(1, k, left1.at[k], second, early_ref.shape[1] // 2)

        @pl.when(step == OFB + OCC_DEV + k)
        def _(k=k):
            multiply(0, k, left0, first, VB // 2)
            if k == OCC_DEV - 1:
                for copy in copies:
                    copy.wait()


def middle(scalars, order, own, other, energies):
    pairs = other.shape[0]
    depth = 2 * OFB * BLK
    rows = VB // 2 * BLK
    raw = pl.BlockSpec(
        (pairs // OFB, EARLY_GROUPS, 8, BLK),
        lambda f, *_: (jnp.minimum(f, OFB - 1), 0, 0, 0),
    )

    def out_block(f, *_):
        turn = jnp.maximum(f - OFB, 0)
        return (lax.rem(turn, OCC_DEV) * PARTNERS + 1 - turn // OCC_DEV, 0, 0)

    return pl.pallas_call(
        middle_kernel,
        grid_spec=pltpu.PrefetchScalarGridSpec(
            num_scalar_prefetch=len(scalars),
            grid=(OFB + OCC_DEV * PARTNERS,),
            in_specs=[
                pl.BlockSpec(order.shape, lambda f, *_: (0, 0)),
                raw,
                raw,
                pl.BlockSpec(energies.shape, lambda f, *_: (0, 0, 0)),
            ],
            out_specs=[
                pl.BlockSpec((1, rows, VB * BLK), out_block),
                pl.BlockSpec(memory_space=pl.ANY),
            ],
            scratch_shapes=[
                pltpu.VMEM((2, OCC_DEV * ODB, OFB, BLK, BLK), BF16),
                pltpu.VMEM((depth, ODB * BLK), BF16),
                pltpu.VMEM((depth, EARLY * BLK), BF16),
                pltpu.VMEM((rows, depth), BF16),
                pltpu.VMEM((OCC_DEV, rows, depth), BF16),
                pltpu.SemaphoreType.DMA((OCC_DEV,)),
            ],
        ),
        out_shape=[
            jax.ShapeDtypeStruct((OCC_DEV * PARTNERS, rows, VB * BLK), BF16),
            jax.ShapeDtypeStruct((OCC_DEV * rows, depth), BF16),
        ],
        compiler_params=pltpu.CompilerParams(vmem_limit_bytes=60 * 1024 * 1024),
        name="middle",
    )(*scalars, order, own, other, energies)


def stage_kernel(from_ref, to_ref, done):
    copies = [
        pltpu.make_async_copy(from_ref.at[part], to_ref.at[part], done.at[n])
        for n, part in enumerate(
            pl.ds(n * from_ref.shape[0] // 4, from_ref.shape[0] // 4) for n in range(4)
        )
    ]
    for copy in copies:
        copy.start()
    for copy in copies:
        copy.wait()


def stage(x):
    return pl.pallas_call(
        stage_kernel,
        in_specs=[pl.BlockSpec(memory_space=pl.ANY)],
        out_specs=pl.BlockSpec(memory_space=pl.ANY),
        out_shape=jax.ShapeDtypeStruct(x.shape, x.dtype),
        scratch_shapes=[pltpu.SemaphoreType.DMA((4,))],
        compiler_params=pltpu.CompilerParams(vmem_limit_bytes=1024 * 1024),
        name="stage",
    )(x)


def late_kernel(
    vir_ref, late_ref, count_ref, occ_ref, aux_ref,
    order_ref, left_ref, own_ref, other_ref, energy_ref, before_ref,
    out_ref, right, tiles, sent,
):
    k = pl.program_id(0)
    p = k * PARTNERS + 1
    group = order_ref.shape[0] // 8
    chunks = own_ref.shape[0] // group

    @pl.when(k == 0)
    def _():
        for h, source in enumerate((own_ref, other_ref)):
            for s in range(0, chunks, 4):
                done = sorted_rows(
                    order_ref[...],
                    [source[(s + i) * group : (s + i + 1) * group] for i in range(4)],
                ).astype(BF16)
                for i in range(4):
                    at = (h * chunks + s + i) * HALF
                    for j in range(4):
                        right[at : at + HALF, j * BLK : (j + 1) * BLK] = done[
                            j * HALF : (j + 1) * HALF, i * BLK : (i + 1) * BLK
                        ]

    base = aux_ref[0] * left_ref.shape[0]
    row_energy = row_energies(energy_ref, p, base, left_ref.shape[0])
    live_count = count_ref[p, 0]

    def each(kk, act):
        q = kk * PARTNERS + 1
        for n in range(LATE):
            v = late_ref[q, n]
            first = late_ref[q, n // 2 * 2]
            new = (v != first) if n % 2 else True
            live = (first < count_ref[q, 0]) & (aux_ref[0] * (VB // 2) < count_ref[q, 0])

            @pl.when(live & new)
            def _(n=n, v=v):
                at = pl.multiple_of(v * BLK, BLK)
                act(pltpu.make_async_copy(
                    tiles.at[kk, n], out_ref.at[q, :, pl.ds(at, BLK)], sent.at[kk, n]
                ))

    for turn in range(LATE // 2):
        leading = late_ref[p, turn * 2]

        @pl.when((leading < live_count) & (aux_ref[0] * (VB // 2) < live_count))
        def _(turn=turn):
            at = [late_ref[p, turn * 2 + n] for n in range(2)]
            columns = [
                pl.multiple_of((vir_ref[p, 1, v] - EARLY) * BLK, BLK) for v in at
            ]
            product = jnp.dot(
                left_ref[...],
                jnp.concatenate([right[:, pl.ds(c, BLK)] for c in columns], axis=1),
                preferred_element_type=F32,
            )
            for n, v in enumerate(at):
                tiles[k, turn * 2 + n] = amplitudes(
                    product[:, n * BLK : (n + 1) * BLK],
                    v, p, count_ref, occ_ref, energy_ref, base, row_energy,
                )

    each(k, lambda copy: copy.start())

    @pl.when(k == pl.num_programs(0) - 1)
    def _():
        for kk in range(OCC_DEV):
            each(kk, lambda copy: copy.wait())


def late_products(scalars, order, left1, own, other, energies, before):
    depth = left1.shape[1]
    rows = left1.shape[0] // OCC_DEV
    out = pl.BlockSpec(memory_space=pl.ANY)
    return pl.pallas_call(
        late_kernel,
        grid_spec=pltpu.PrefetchScalarGridSpec(
            num_scalar_prefetch=len(scalars),
            grid=(OCC_DEV,),
            in_specs=[
                pl.BlockSpec(order.shape, lambda k, *_: (0, 0)),
                pl.BlockSpec((rows, depth), lambda k, *_: (k, 0)),
                pl.BlockSpec(own.shape, lambda k, *_: (0, 0, 0)),
                pl.BlockSpec(other.shape, lambda k, *_: (0, 0, 0)),
                pl.BlockSpec(energies.shape, lambda k, *_: (0, 0, 0)),
                out,
            ],
            out_specs=out,
            scratch_shapes=[
                pltpu.VMEM((depth, LATE * BLK), BF16),
                pltpu.VMEM((OCC_DEV, LATE, rows, BLK), BF16),
                pltpu.SemaphoreType.DMA((OCC_DEV, LATE)),
            ],
        ),
        out_shape=jax.ShapeDtypeStruct(before.shape, BF16),
        input_output_aliases={len(scalars) + 5: 0},
        compiler_params=pltpu.CompilerParams(vmem_limit_bytes=32 * 1024 * 1024),
        name="late",
    )(*scalars, order, left1, own, other, energies, before)


def per_device(
    three_index, partners, vir_blocks, fit_blocks, block_counts, virt_energies, occ_energies
):
    owners = lax.axis_size("occ")
    owner = lax.axis_index("occ")
    aux = lax.axis_index("aux").reshape(1)
    pairs_dev = OCC_DEV * PARTNERS

    def swap(x):
        return lax.ppermute(x, "aux", [(0, 1), (1, 0)])

    rows = jnp.transpose(three_index[0], (1, 0, 2))
    orbitals = jnp.arange(rows.shape[1], dtype=jnp.int32)
    wanted = jnp.concatenate(
        [orbitals.reshape(owners, OCC_DEV).T.reshape(-1), partners.reshape(owners, PARTNERS).T.reshape(-1)]
    )
    pick = (wanted[:, None] == orbitals[None, :]).astype(BF16)
    early, late = pack(pick, rows, owners)
    early = lax.all_to_all(early, "occ", 0, 0, tiled=True)
    late = lax.all_to_all(late, "occ", 0, 0, tiled=True)

    fit_own = fit_blocks[:, :, 0, :]
    fits = jnp.stack([fit_own, swap(fit_own)])
    vir = lax.dynamic_slice_in_dim(vir_blocks, owner * pairs_dev, pairs_dev, 0)
    numbers = jnp.arange(VB, dtype=jnp.int32)
    is_late = vir[:, 1, :] >= EARLY

    def listed(flags, length):
        upto = numbers[None, :] <= numbers[:, None]
        rank = jnp.sum(jnp.where(flags[:, None, :] & upto, 1, 0), axis=2)
        total = rank[:, -1:]
        index = jnp.arange(1, length + 1, dtype=jnp.int32)
        nth = jnp.minimum(index, total)
        hit = flags[:, None, :] & (rank[:, None, :] == nth[:, :, None])
        found = jnp.sum(jnp.where(hit, numbers, 0), axis=2)
        return jnp.where(index <= total + total % 2, found, VB)

    early_at = listed(~is_late, EARLY + 1)
    late_at = listed(is_late, LATE)
    mine = lax.dynamic_slice_in_dim(occ_energies, owner * OCC_DEV, OCC_DEV, 0)
    partner_ids = lax.dynamic_slice_in_dim(partners, owner * PARTNERS, PARTNERS, 0)
    theirs = jnp.sum(
        jnp.where(partner_ids[:, None] == orbitals[None, :], occ_energies[None, :], 0.0), axis=1
    )
    occ_pair = jnp.stack([jnp.repeat(mine, PARTNERS), jnp.concatenate([theirs] * OCC_DEV)])
    energies = virt_energies[:, None, :]

    place = jnp.arange(256, dtype=jnp.int32)
    source = (place % HALF) // 2 * 8 + (place // HALF) * 2 + place % 2
    order = (source[:, None] == place[None, :]).astype(BF16)

    early = early.reshape(owners * ROWP, EARLY_GROUPS, 8, BLK)
    scalars = (vir, fits, block_counts, occ_pair, aux, early_at)
    out, left1 = middle(scalars, order, early, swap(early), energies)
    late, out = lax.optimization_barrier((late, out))
    late = late.reshape(owners * ROWP, 8, BLK)
    scalars = (vir, late_at, block_counts, occ_pair, aux)
    return late_products(scalars, order, stage(left1), late, swap(late), energies, out)


def solution(mesh):
    return jax.shard_map(
        per_device,
        mesh=mesh,
        in_specs=(
            P("aux", None, "occ", None),
            P(),
            P(),
            P("occ", None, "aux", None),
            P("occ", None),
            P("occ", None),
            P(),
        ),
        out_specs=P("occ", "aux", None),
        check_vma=False,
    )
```
